32 devices in a mesh: pert: 4 (over z), gene: 8 (over y, x, core).
Axes of the slice: x: 2, y: 2, z: 4, core: 2. Of those that a mesh axis runs over, the one named last changes fastest.
Arguments:
- tensor: bfloat16 [4096, 8, 4096], P('pert', None, 'gene'), may hold values from -2400 to 2400
- pert_factor: bfloat16 [4096, 128], P('pert'), may hold values from -10 to 10
- context_factor: bfloat16 [8, 128], replicated, may hold values from -3 to 3
Outputs:
- gene_factor: bfloat16 [4096, 128], P('gene')
- pert_updated: bfloat16 [4096, 128], P('pert')
The draws below stay inside these ranges and needn't reach their ends.
All inputs are finite; a program needn't handle non-finite values.
Results may differ from the reference program's by a relative error of at most 0.0042.
Values may be sent and summed in bfloat16 or wider, within the bound.
A program may use at most 64 MiB of HBM per device.

```python
import math
import jax
import jax.numpy as jnp
from jax import lax

R = 128
K = 8
I_DEV = 1024
J_DEV = 512
PERTS = 4096
GENES = 4096
N_PERT = 4
N_GENE = 8


def draw_pert_factor(key, part):
    key_scale, key_base = jax.random.split(key, 2)
    scales = jnp.exp(jax.random.uniform(key_scale, (PERTS, 1), jnp.float32, math.log(0.3), math.log(3.0)))
    values = jax.random.normal(key_base, (PERTS, R), jnp.float32) * scales
    return jnp.clip(values, -10.0, 10.0).astype(jnp.bfloat16)


def draw_tensor(key, part):
    key_rough, key_values = jax.random.split(jax.random.fold_in(key, 17), 2)
    place = jnp.arange(GENES, dtype=jnp.float32) / GENES
    rough = jnp.exp(jax.random.uniform(key_rough, (GENES,), jnp.float32, 0.0, math.log(4.0)))
    column_scale = 32.0 * jnp.exp(math.log(3.0) * place) * rough
    values = jnp.clip(jax.random.normal(key_values, (PERTS, K, GENES), jnp.float32), -6.0, 6.0)
    return (values * column_scale[None, None, :]).astype(jnp.bfloat16)


def gaussian(stream_key, dims, scale, bound, held_as=jnp.bfloat16):
    return jnp.clip(scale * jax.random.normal(stream_key, dims, jnp.float32), -bound, bound).astype(held_as)


def setup_inputs(seed: int = 0) -> dict:
    streams_of = jax.random.split(jax.random.key(seed), 4)
    tensor = draw_tensor(jax.random.fold_in(streams_of[3], 71), 0)
    pert_factor = draw_pert_factor(jax.random.fold_in(streams_of[3], 71), 0)
    context_factor = gaussian(streams_of[2], (K, R), 0.6, 3.0)
    return {"tensor": tensor, "pert_factor": pert_factor, "context_factor": context_factor}


epsilon = 1e-06

def solve_gram(rhs, gram):
    lower = jnp.linalg.cholesky(gram)
    half = lax.linalg.triangular_solve(lower, rhs, left_side=False, lower=True, transpose_a=True)
    return lax.linalg.triangular_solve(lower, half, left_side=False, lower=True, transpose_a=False)

def reference(tensor, pert_factor, context_factor):
    context32 = context_factor.astype(jnp.float32)
    gram_b = jnp.dot(context_factor.T.astype(jnp.float32), context_factor.astype(jnp.float32), preferred_element_type=jnp.float32)
    gram_a = jnp.dot(pert_factor.T.astype(jnp.float32), pert_factor.astype(jnp.float32), preferred_element_type=jnp.float32)
    tensor_blocks = tensor.reshape(N_PERT, I_DEV, K, J_DEV * N_GENE)
    factor_blocks = pert_factor.reshape(N_PERT, I_DEV, R)

    def gene_step(summed, blocks_pair):
        tensor_block, factor_block = blocks_pair
        partial_sum = jnp.einsum('ikj,ir->kjr', tensor_block.astype(jnp.float32), factor_block.astype(jnp.float32))
        return (summed + partial_sum, None)
    summed, unused = lax.scan(gene_step, jnp.zeros((K, J_DEV * N_GENE, R), jnp.float32), (tensor_blocks, factor_blocks))
    mttkrp_c = lax.optimization_barrier(jnp.sum(summed * context32[:, None, :], axis=0))
    solved_c = solve_gram(mttkrp_c, gram_a * gram_b)
    gram_s = jnp.dot(solved_c.T.astype(jnp.float32), solved_c.astype(jnp.float32), precision=lax.Precision.HIGHEST, preferred_element_type=jnp.float32)
    scale_c = jnp.sqrt(jnp.diagonal(gram_s) / (J_DEV * N_GENE) + epsilon)
    gene_factor = (solved_c / scale_c[None, :]).astype(jnp.bfloat16)
    gram_c = gram_s / (scale_c[:, None] * scale_c[None, :])
    gene32 = gene_factor.astype(jnp.float32)

    def pert_block(tensor_block):
        partial_sum = jnp.einsum('ikj,jr->ikr', tensor_block.astype(jnp.float32), gene32)
        return lax.optimization_barrier(jnp.sum(partial_sum * context32[None, :, :], axis=1))
    mttkrp_a = lax.map(pert_block, tensor_blocks).reshape(N_PERT * I_DEV, R)
    solved_a = solve_gram(mttkrp_a, gram_c * gram_b)
    scale_a = jnp.sqrt(lax.optimization_barrier(jnp.mean(solved_a * solved_a, axis=0)) + epsilon)
    pert_updated = (solved_a / scale_a[None, :]).astype(jnp.bfloat16)
    return (gene_factor, pert_updated)
```

```python
import functools

import jax
import jax.numpy as jnp
from jax import lax
from jax.experimental import pallas as pl
from jax.experimental.pallas import tpu as pltpu
from jax.sharding import PartitionSpec as P

epsilon = 1e-06
MESH = pl.DeviceIdType.MESH
HIGHEST = lax.Precision.HIGHEST
PANEL = 8


def dot32(a, b, dims):
    return lax.dot_general(
        a, b, (dims, ((), ())), precision=HIGHEST, preferred_element_type=jnp.float32
    )


def invert_steps(a, steps):
    size = a.shape[0]
    lane = lax.broadcasted_iota(jnp.int32, (PANEL, size), 1)
    row = lax.broadcasted_iota(jnp.int32, (PANEL, size), 0)
    full_lane = lax.broadcasted_iota(jnp.int32, (size, size), 1)

    def step(_, a):
        panel = a[:PANEL]
        columns = [jnp.broadcast_to(panel[:, j : j + 1], (PANEL, size)) for j in range(PANEL)]
        for k in range(PANEL):
            inverse = 1.0 / columns[k][k : k + 1]
            pivot = jnp.where(lane[:1] == k, inverse, panel[k : k + 1] * inverse)
            kept = jnp.where(lane == k, 0.0, panel)
            panel = jnp.where(row == k, pivot, kept - columns[k] * pivot)
            for j in range(k + 1, PANEL):
                head = columns[j][k : k + 1] * inverse
                columns[j] = jnp.where(row == k, head, columns[j] - columns[k] * head)
        shift = size - PANEL
        turned = pltpu.roll(panel, shift, 1)
        rest = a[PANEL:]
        out = pltpu.roll(jnp.where(full_lane[PANEL:] < PANEL, 0.0, rest), shift, 1)
        for j in range(PANEL):
            out = out - rest[:, j : j + 1] * turned[j : j + 1]
        return jnp.concatenate([out, turned], axis=0)

    return lax.fori_loop(0, steps, step, a)


def sweep(
    n_pert, n_gene, tensor_hbm, factor_ref, context_ref, gene_ref, pert_ref,
    tensor, khatri, product, slab_send, gram_z, gram_g, matrix, mttkrp_part, mttkrp_in, mttkrp_all,
    second_part, second_in, squares_g, squares_z, final, load_sem,
    z_send, z_recv, g_send, g_recv,
):
    z = lax.axis_index("pert")
    g = lax.axis_index("gene")
    rows_i, rank = factor_ref.shape
    contexts = context_ref.shape[0]
    depth, rows_j = tensor.shape
    own_j = rows_j // n_pert
    own_i = rows_i // n_gene
    slab = rank // n_gene
    blocks, width = load_sem.shape[0], rows_j // load_sem.shape[0]
    per_block = width // own_j
    gene_count = rows_j * n_gene
    pert_count = rows_i * n_pert

    def z_copy(stage, src, dst, peer):
        return pltpu.make_async_remote_copy(
            src_ref=src, dst_ref=dst.at[z], send_sem=z_send.at[stage, peer],
            recv_sem=z_recv.at[stage, z], device_id=(peer, g), device_id_type=MESH,
        )

    def g_copy(stage, src, dst, peer):
        return pltpu.make_async_remote_copy(
            src_ref=src, dst_ref=dst.at[g], send_sem=g_send.at[stage, peer],
            recv_sem=g_recv.at[stage, g], device_id=(z, peer), device_id_type=MESH,
        )

    def z_wait(stage, dst):
        for d in range(1, n_pert):
            peer = lax.rem(z + d, n_pert)
            pltpu.make_async_remote_copy(
                src_ref=dst.at[peer], dst_ref=dst.at[peer], send_sem=z_send.at[stage, peer],
                recv_sem=z_recv.at[stage, peer], device_id=(peer, g), device_id_type=MESH,
            ).wait_recv()

    def g_wait(stage, dst):
        for d in range(1, n_gene):
            peer = lax.rem(g + d, n_gene)
            pltpu.make_async_remote_copy(
                src_ref=dst.at[peer], dst_ref=dst.at[peer], send_sem=g_send.at[stage, peer],
                recv_sem=g_recv.at[stage, peer], device_id=(z, peer), device_id_type=MESH,
            ).wait_recv()

    z_peers = [lax.rem(z + d, n_pert) for d in range(1, n_pert)]
    g_peers = [lax.rem(g + d, n_gene) for d in range(1, n_gene)]
    sent = []

    def send(copy):
        copy.start()
        sent.append(copy)

    barrier = pltpu.get_barrier_semaphore()
    for peer in z_peers:
        pl.semaphore_signal(barrier, inc=1, device_id=(peer, g), device_id_type=MESH)
    for peer in g_peers:
        pl.semaphore_signal(barrier, inc=1, device_id=(z, peer), device_id_type=MESH)

    def load(block):
        columns = pl.ds(pl.multiple_of(block * width, width), width)
        return pltpu.make_async_copy(
            tensor_hbm.at[:, columns], tensor.at[:, columns], load_sem.at[block]
        )

    order = [lax.rem(z // per_block + 1 + t, blocks) for t in range(blocks)]
    for block in order:
        load(block).start()

    factor = factor_ref[...]
    context = context_ref[...]
    context32 = context.astype(jnp.float32)
    gram_b = lax.dot_general(
        context, context, (((0,), (0,)), ((), ())), preferred_element_type=jnp.float32
    )
    gram = lax.dot_general(
        factor, factor, (((0,), (0,)), ((), ())), preferred_element_type=jnp.float32
    )
    for s in range(n_gene):
        slab_send[s] = gram[s * slab : (s + 1) * slab]
    pl.semaphore_wait(barrier, n_pert + n_gene - 2)

    gram_z[z] = slab_send[g]
    for peer in z_peers:
        send(z_copy(0, gram_z.at[z], gram_z, peer))

    step_i = 128

    def build(t, carry):
        part = factor_ref[pl.ds(pl.multiple_of(t * step_i, step_i), step_i), :]
        both = part.astype(jnp.float32)[:, None, :] * context32[None]
        both = both.reshape(step_i * contexts, rank)
        high = both.astype(jnp.bfloat16)
        low = (both - high.astype(jnp.float32)).astype(jnp.bfloat16)
        here = pl.ds(pl.multiple_of(t * step_i * contexts, step_i * contexts), step_i * contexts)
        khatri[here, :rank] = high
        khatri[here, rank:] = low
        return carry

    lax.fori_loop(0, rows_i // step_i, build, 0)

    z_wait(0, gram_z)
    total = gram_z[0]
    for s in range(1, n_pert):
        total = total + gram_z[s]
    gram_g[g] = total
    for peer in g_peers:
        send(g_copy(0, gram_g.at[g], gram_g, peer))

    step_d = 2048
    for t, block in enumerate(order):
        load(block).wait()
        columns = pl.ds(pl.multiple_of(block * width, width), width)
        product[...] = jnp.zeros_like(product)

        def multiply(c, carry):
            here = pl.ds(pl.multiple_of(c * step_d, step_d), step_d)
            product[...] += lax.dot_general(
                khatri[here, :], tensor[here, columns], (((0,), (0,)), ((), ())),
                preferred_element_type=jnp.float32,
            )
            return carry

        lax.fori_loop(0, depth // step_d, multiply, 0)
        turned = (product[:rank] + product[rank:]).T
        for q in range(per_block):
            owner = block * per_block + q
            mttkrp_part[owner] = turned[q * own_j : (q + 1) * own_j]

            @pl.when(owner != z)
            def _():
                z_copy(1, mttkrp_part.at[owner], mttkrp_in, owner).start()

    mttkrp_in[z] = mttkrp_part[z]
    for peer in z_peers:
        sent.append(z_copy(1, mttkrp_part.at[peer], mttkrp_in, peer))

    g_wait(0, gram_g)
    for s in range(n_gene):
        matrix[s * slab : (s + 1) * slab, :] = gram_g[s]
    steps = rank // PANEL
    early = steps // 4
    inverse = invert_steps(matrix[...] * gram_b, early)

    z_wait(1, mttkrp_in)
    total = mttkrp_in[0]
    for s in range(1, n_pert):
        total = total + mttkrp_in[s]
    mttkrp_all[z] = total
    for peer in z_peers:
        send(z_copy(2, mttkrp_all.at[z], mttkrp_all, peer))

    inverse = invert_steps(inverse, steps - early)
    z_wait(2, mttkrp_all)
    solved = dot32(mttkrp_all[...].reshape(rows_j, rank), inverse, ((1,), (0,)))
    gram = dot32(solved, solved, ((0,), (0,)))
    for s in range(n_gene):
        second_gram = gram[s * slab : (s + 1) * slab]
        slab_send[s] = second_gram

    gram_in, gram_out = gram_g.at[n_gene : 2 * n_gene], gram_g.at[2 * n_gene : 3 * n_gene]
    gram_in[g] = slab_send[g]
    for peer in g_peers:
        send(g_copy(1, slab_send.at[peer], gram_in, peer))
    g_wait(1, gram_in)
    total = gram_in[0]
    for s in range(1, n_gene):
        total = total + gram_in[s]
    gram_out[g] = total
    for peer in g_peers:
        send(g_copy(2, gram_out.at[g], gram_out, peer))
    g_wait(2, gram_out)
    for s in range(n_gene):
        matrix[s * slab : (s + 1) * slab, :] = gram_out[s]
    gram_s = matrix[...]

    diagonal = lax.broadcasted_iota(jnp.int32, (rank, rank), 0) == lax.broadcasted_iota(
        jnp.int32, (rank, rank), 1
    )
    on_diagonal = jnp.where(diagonal, gram_s, 0.0)
    scale_row = jnp.sqrt(jnp.sum(on_diagonal, axis=0, keepdims=True) / gene_count + epsilon)
    scale_column = jnp.sqrt(jnp.sum(on_diagonal, axis=1, keepdims=True) / gene_count + epsilon)
    gene_factor = (solved / scale_row).astype(jnp.bfloat16)
    gene_ref[...] = gene_factor
    gram_pert_mode = gram_s / (scale_column * scale_row) * gram_b

    def second(peer):
        here = pl.ds(pl.multiple_of(peer * own_i * contexts, own_i * contexts), own_i * contexts)
        partial = jnp.dot(tensor[here, :], gene_ref[...], preferred_element_type=jnp.float32)
        return jnp.sum(partial.reshape(own_i, contexts, rank) * context32[None], axis=1)

    def second_step(t, carry):
        peer = lax.rem(g + 1 + t, n_gene)
        second_part[peer] = second(peer)
        g_copy(3, second_part.at[peer], second_in, peer).start()
        return carry

    lax.fori_loop(0, n_gene - 1, second_step, 0)
    second_in[g] = second(g)
    for peer in g_peers:
        sent.append(g_copy(3, second_part.at[peer], second_in, peer))

    inverse = invert_steps(gram_pert_mode, steps)
    g_wait(3, second_in)
    total = second_in[0]
    for s in range(1, n_gene):
        total = total + second_in[s]
    solved = dot32(total, inverse, ((1,), (0,)))

    squares_g[g] = jnp.sum((solved * solved).reshape(own_i // 8, 8, rank), axis=0)
    for peer in g_peers:
        send(g_copy(4, squares_g.at[g], squares_g, peer))
    g_wait(4, squares_g)
    total = squares_g[0]
    for s in range(1, n_gene):
        total = total + squares_g[s]
    squares_z[z] = total
    for peer in z_peers:
        send(z_copy(3, squares_z.at[z], squares_z, peer))
    z_wait(3, squares_z)
    total = squares_z[0]
    for s in range(1, n_pert):
        total = total + squares_z[s]
    scale = jnp.sqrt(jnp.sum(total, axis=0, keepdims=True) / pert_count + epsilon)
    final[g] = (solved / scale).astype(jnp.bfloat16)
    for peer in g_peers:
        send(g_copy(5, final.at[g], final, peer))
    g_wait(5, final)
    for s in range(n_gene):
        pert_ref[s * own_i : (s + 1) * own_i, :] = final[s]
    for copy in sent:
        copy.wait_send()


def shards(n_pert, n_gene, tensor, pert_factor, context_factor):
    rows_i, contexts, rows_j = tensor.shape
    rank = pert_factor.shape[1]
    own_j, own_i, slab = rows_j // n_pert, rows_i // n_gene, rank // n_gene
    depth = rows_i * contexts
    width = 256
    f32, bf16 = jnp.float32, jnp.bfloat16
    vmem = pl.BlockSpec(memory_space=pltpu.VMEM)
    return pl.pallas_call(
        functools.partial(sweep, n_pert, n_gene),
        out_shape=(
            jax.ShapeDtypeStruct((rows_j, rank), bf16),
            jax.ShapeDtypeStruct((rows_i, rank), bf16),
        ),
        in_specs=[pl.BlockSpec(memory_space=pl.ANY), vmem, vmem],
        out_specs=(vmem, vmem),
        scratch_shapes=[
            pltpu.VMEM((depth, rows_j), bf16),
            pltpu.VMEM((depth, 2 * rank), bf16),
            pltpu.VMEM((2 * rank, width), f32),
            pltpu.VMEM((n_gene, slab, rank), f32),
            pltpu.VMEM((n_pert, slab, rank), f32),
            pltpu.VMEM((3 * n_gene, slab, rank), f32),
            pltpu.VMEM((rank, rank), f32),
            pltpu.VMEM((n_pert, own_j, rank), f32),
            pltpu.VMEM((n_pert, own_j, rank), f32),
            pltpu.VMEM((n_pert, own_j, rank), f32),
            pltpu.VMEM((n_gene, own_i, rank), f32),
            pltpu.VMEM((n_gene, own_i, rank), f32),
            pltpu.VMEM((n_gene, 8, rank), f32),
            pltpu.VMEM((n_pert, 8, rank), f32),
            pltpu.VMEM((n_gene, own_i, rank), bf16),
            pltpu.SemaphoreType.DMA((rows_j // width,)),
            pltpu.SemaphoreType.DMA((4, n_pert)),
            pltpu.SemaphoreType.DMA((4, n_pert)),
            pltpu.SemaphoreType.DMA((6, n_gene)),
            pltpu.SemaphoreType.DMA((6, n_gene)),
        ],
        compiler_params=pltpu.CompilerParams(
            collective_id=0, has_side_effects=True, vmem_limit_bytes=48 * 1024 * 1024
        ),
        name="sweep",
    )(tensor.reshape(depth, rows_j), pert_factor, context_factor)


def solution(mesh):
    return jax.shard_map(
        functools.partial(shards, mesh.shape["pert"], mesh.shape["gene"]),
        mesh=mesh,
        in_specs=(P("pert", None, "gene"), P("pert", None), P()),
        out_specs=(P("gene", None), P("pert", None)),
        check_vma=False,
    )
```

```python
import functools

import jax
import jax.numpy as jnp
from jax import lax
from jax.experimental import pallas as pl
from jax.experimental.pallas import tpu as pltpu
from jax.sharding import PartitionSpec as P

epsilon = 1e-06
MESH = pl.DeviceIdType.MESH
HIGHEST = lax.Precision.HIGHEST
PANEL = 8


def dot32(a, b, dims):
    return lax.dot_general(
        a, b, (dims, ((), ())), precision=HIGHEST, preferred_element_type=jnp.float32
    )


def reciprocal(x):
    r = pl.reciprocal(x, approx=True)
    r = r * (2.0 - x * r)
    return r * (2.0 - x * r)


def invert_step(a):
    size = a.shape[0]
    lane = lax.broadcasted_iota(jnp.int32, (PANEL, size), 1)
    row = lax.broadcasted_iota(jnp.int32, (PANEL, size), 0)
    rest_lane = lax.broadcasted_iota(jnp.int32, (size - PANEL, size), 1)
    panel = a[:PANEL]
    columns = [jnp.broadcast_to(panel[:, j : j + 1], (PANEL, size)) for j in range(PANEL)]
    for k in range(PANEL):
        inverse = reciprocal(columns[k][k : k + 1])
        pivot = jnp.where(lane[k : k + 1] == k, inverse, panel[k : k + 1] * inverse)
        kept = jnp.where(lane == k, 0.0, panel)
        panel = jnp.where(row == k, pivot, kept - columns[k] * pivot)
        for j in range(k + 1, PANEL):
            head = columns[j][k : k + 1] * inverse
            columns[j] = jnp.where(row == k, head, columns[j] - columns[k] * head)
    shift = size - PANEL
    turned = pltpu.roll(panel, shift, 1)
    rest = a[PANEL:]
    out = pltpu.roll(jnp.where(rest_lane < PANEL, 0.0, rest), shift, 1)
    for j in range(PANEL):
        out = out - rest[:, j : j + 1] * turned[j : j + 1]
    return jnp.concatenate([out, turned], axis=0)


def invert_steps(a, steps):
    return lax.fori_loop(0, steps, lambda _, a: invert_step(a), a)


def sweep(
    n_pert, n_gene, tensor_hbm, factor_hbm, context_hbm, gene_ref, pert_ref,
    factor_ref, context_ref, tensor, khatri, product, slab_send, gram_z, gram_g, matrix,
    mttkrp_part, mttkrp_in, gene_all,
    second_part, second_in, squares_g, squares_z, final, load_sem, small_sem,
    z_send, z_recv, g_send, g_recv,
):
    z = lax.axis_index("pert")
    g = lax.axis_index("gene")
    rows_i, rank = factor_ref.shape
    contexts = context_ref.shape[0]
    depth, rows_j = tensor.shape
    own_j = rows_j // n_pert
    own_i = rows_i // n_gene
    slab = rank // n_gene
    blocks, width = load_sem.shape[0], rows_j // load_sem.shape[0]
    per_block = width // own_j
    gene_count = rows_j * n_gene
    pert_count = rows_i * n_pert

    def z_copy(stage, src, dst, peer):
        return pltpu.make_async_remote_copy(
            src_ref=src, dst_ref=dst.at[z], send_sem=z_send.at[stage, peer],
            recv_sem=z_recv.at[stage, z], device_id=(peer, g), device_id_type=MESH,
        )

    def g_copy(stage, src, dst, peer):
        return pltpu.make_async_remote_copy(
            src_ref=src, dst_ref=dst.at[g], send_sem=g_send.at[stage, peer],
            recv_sem=g_recv.at[stage, g], device_id=(z, peer), device_id_type=MESH,
        )

    def z_wait(stage, dst):
        for d in range(1, n_pert):
            peer = lax.rem(z + d, n_pert)
            pltpu.make_async_remote_copy(
                src_ref=dst.at[peer], dst_ref=dst.at[peer], send_sem=z_send.at[stage, peer],
                recv_sem=z_recv.at[stage, peer], device_id=(peer, g), device_id_type=MESH,
            ).wait_recv()

    def g_wait(stage, dst):
        for d in range(1, n_gene):
            peer = lax.rem(g + d, n_gene)
            pltpu.make_async_remote_copy(
                src_ref=dst.at[peer], dst_ref=dst.at[peer], send_sem=g_send.at[stage, peer],
                recv_sem=g_recv.at[stage, peer], device_id=(z, peer), device_id_type=MESH,
            ).wait_recv()

    z_peers = [lax.rem(z + d, n_pert) for d in range(1, n_pert)]
    g_peers = [lax.rem(g + d, n_gene) for d in range(1, n_gene)]
    sent = []

    def send(copy):
        copy.start()
        sent.append(copy)

    barrier = pltpu.get_barrier_semaphore()
    for peer in z_peers:
        pl.semaphore_signal(barrier, inc=1, device_id=(peer, g), device_id_type=MESH)
    for peer in g_peers:
        pl.semaphore_signal(barrier, inc=1, device_id=(z, peer), device_id_type=MESH)

    def load(block):
        columns = pl.ds(pl.multiple_of(block * width, width), width)
        return pltpu.make_async_copy(
            tensor_hbm.at[:, columns], tensor.at[:, columns], load_sem.at[block]
        )

    order = [lax.rem(z // per_block + 1 + t, blocks) for t in range(blocks)]
    small = [
        pltpu.make_async_copy(factor_hbm, factor_ref, small_sem.at[0]),
        pltpu.make_async_copy(context_hbm, context_ref, small_sem.at[1]),
    ]
    for copy in small:
        copy.start()
    for block in order:
        load(block).start()
    for copy in small:
        copy.wait()

    factor = factor_ref[...]
    context = context_ref[...]
    context32 = context.astype(jnp.float32)
    gram_b = lax.dot_general(
        context, context, (((0,), (0,)), ((), ())), preferred_element_type=jnp.float32
    )
    gram = lax.dot_general(
        factor, factor, (((0,), (0,)), ((), ())), preferred_element_type=jnp.float32
    )
    for s in range(n_gene):
        slab_send[s] = gram[s * slab : (s + 1) * slab]
    pl.semaphore_wait(barrier, n_pert + n_gene - 2)

    gram_z[z] = slab_send[g]
    for peer in z_peers:
        send(z_copy(0, gram_z.at[z], gram_z, peer))

    step_i = 128
    step_p = step_i * contexts
    repeat = (
        lax.broadcasted_iota(jnp.int32, (step_i, step_p), 1) // contexts
        == lax.broadcasted_iota(jnp.int32, (step_i, step_p), 0)
    ).astype(jnp.bfloat16)
    cycle = (
        lax.rem(lax.broadcasted_iota(jnp.int32, (contexts, step_p), 1), contexts)
        == lax.broadcasted_iota(jnp.int32, (contexts, step_p), 0)
    ).astype(jnp.bfloat16)
    context_rows = lax.dot_general(
        context, cycle, (((0,), (0,)), ((), ())), preferred_element_type=jnp.float32
    )

    for t in range(rows_i // step_i):
        both = context_rows * lax.dot_general(
            factor_ref[t * step_i : (t + 1) * step_i, :], repeat, (((0,), (0,)), ((), ())),
            preferred_element_type=jnp.float32,
        )
        high = both.astype(jnp.bfloat16)
        khatri[:rank, t * step_p : (t + 1) * step_p] = high
        khatri[rank:, t * step_p : (t + 1) * step_p] = (
            both - high.astype(jnp.float32)
        ).astype(jnp.bfloat16)

    z_wait(0, gram_z)
    total = gram_z[0]
    for s in range(1, n_pert):
        total = total + gram_z[s]
    gram_g[g] = total
    for peer in g_peers:
        send(g_copy(0, gram_g.at[g], gram_g, peer))

    step_d = 2048
    chunks = depth // step_d
    steps = rank // PANEL
    early = min(2, steps // chunks)

    def multiply(c, columns):
        here = pl.ds(pl.multiple_of(c * step_d, step_d), step_d)
        product[...] += jnp.dot(
            khatri[:, here], tensor[here, columns], preferred_element_type=jnp.float32
        )

    for t, block in enumerate(order):
        load(block).wait()
        columns = pl.ds(pl.multiple_of(block * width, width), width)
        product[...] = jnp.zeros_like(product)
        if t < blocks - 1:
            lax.fori_loop(0, chunks, lambda c, carry: (multiply(c, columns), carry)[1], 0)
        else:
            g_wait(0, gram_g)
            for s in range(n_gene):
                matrix[s * slab : (s + 1) * slab, :] = gram_g[s]

            def both_steps(c, inverse):
                multiply(c, columns)
                for _ in range(early):
                    inverse = invert_step(inverse)
                return inverse

            inverse = lax.fori_loop(0, chunks, both_steps, matrix[...] * gram_b)
        turned = (product[:rank] + product[rank:]).T
        for q in range(per_block):
            owner = block * per_block + q
            mttkrp_part[owner] = turned[q * own_j : (q + 1) * own_j]

            @pl.when(owner != z)
            def _():
                z_copy(1, mttkrp_part.at[owner], mttkrp_in, owner).start()

    mttkrp_in[z] = mttkrp_part[z]
    for peer in z_peers:
        sent.append(z_copy(1, mttkrp_part.at[peer], mttkrp_in, peer))

    inverse = invert_steps(inverse, steps - early * chunks)
    z_wait(1, mttkrp_in)
    total = mttkrp_in[0]
    for s in range(1, n_pert):
        total = total + mttkrp_in[s]
    solved = dot32(total, inverse, ((1,), (0,)))
    gram = dot32(solved, solved, ((0,), (0,)))
    for s in range(n_gene):
        slab_send[s] = gram[s * slab : (s + 1) * slab]

    gram_in, gram_out = gram_g.at[n_gene : 2 * n_gene], gram_g.at[2 * n_gene : 3 * n_gene]
    gram_in[g] = slab_send[g]
    for peer in g_peers:
        send(g_copy(1, slab_send.at[peer], gram_in, peer))
    g_wait(1, gram_in)
    total = gram_in[0]
    for s in range(1, n_gene):
        total = total + gram_in[s]
    slab_z = gram_z.at[n_pert : 2 * n_pert]
    slab_z[z] = total
    for peer in z_peers:
        send(z_copy(2, slab_z.at[z], slab_z, peer))
    z_wait(2, slab_z)
    total = slab_z[0]
    for s in range(1, n_pert):
        total = total + slab_z[s]
    gram_out[g] = total
    for peer in g_peers:
        send(g_copy(2, gram_out.at[g], gram_out, peer))
    g_wait(2, gram_out)
    for s in range(n_gene):
        matrix[s * slab : (s + 1) * slab, :] = gram_out[s]
    gram_s = matrix[...]

    diagonal = lax.broadcasted_iota(jnp.int32, (rank, rank), 0) == lax.broadcasted_iota(
        jnp.int32, (rank, rank), 1
    )
    on_diagonal = jnp.where(diagonal, gram_s, 0.0)
    scale_row = jnp.sqrt(jnp.sum(on_diagonal, axis=0, keepdims=True) / gene_count + epsilon)
    scale_column = jnp.sqrt(jnp.sum(on_diagonal, axis=1, keepdims=True) / gene_count + epsilon)
    gene_all[z] = (solved / scale_row).astype(jnp.bfloat16)
    for peer in z_peers:
        send(z_copy(4, gene_all.at[z], gene_all, peer))
    gram_pert_mode = gram_s / (scale_column * scale_row) * gram_b

    z_wait(4, gene_all)
    for s in range(n_pert):
        gene_ref[s * own_j : (s + 1) * own_j, :] = gene_all[s]

    def second(peer):
        here = pl.ds(pl.multiple_of(peer * own_i * contexts, own_i * contexts), own_i * contexts)
        partial = jnp.dot(tensor[here, :], gene_ref[...], preferred_element_type=jnp.float32)
        return jnp.sum(partial.reshape(own_i, contexts, rank) * context32[None], axis=1)

    beside = steps // n_gene

    def second_step(t, inverse):
        peer = lax.rem(g + 1 + t, n_gene)
        second_part[peer] = second(peer)
        g_copy(3, second_part.at[peer], second_in, peer).start()
        for _ in range(beside):
            inverse = invert_step(inverse)
        return inverse

    inverse = lax.fori_loop(0, n_gene - 1, second_step, gram_pert_mode)
    second_in[g] = second(g)
    for peer in g_peers:
        sent.append(g_copy(3, second_part.at[peer], second_in, peer))
    inverse = invert_steps(inverse, steps - beside * (n_gene - 1))
    g_wait(3, second_in)
    total = second_in[0]
    for s in range(1, n_gene):
        total = total + second_in[s]
    solved = dot32(total, inverse, ((1,), (0,)))

    squares_g[g] = jnp.sum((solved * solved).reshape(own_i // 8, 8, rank), axis=0)
    for peer in g_peers:
        send(g_copy(4, squares_g.at[g], squares_g, peer))
    g_wait(4, squares_g)
    total = squares_g[0]
    for s in range(1, n_gene):
        total = total + squares_g[s]
    squares_z[z] = total
    for peer in z_peers:
        send(z_copy(3, squares_z.at[z], squares_z, peer))
    z_wait(3, squares_z)
    total = squares_z[0]
    for s in range(1, n_pert):
        total = total + squares_z[s]
    scale = jnp.sqrt(jnp.sum(total, axis=0, keepdims=True) / pert_count + epsilon)
    final[g] = (solved / scale).astype(jnp.bfloat16)
    for peer in g_peers:
        send(g_copy(5, final.at[g], final, peer))
    g_wait(5, final)
    for s in range(n_gene):
        pert_ref[s * own_i : (s + 1) * own_i, :] = final[s]
    for copy in sent:
        copy.wait_send()


def shards(n_pert, n_gene, tensor, pert_factor, context_factor):
    rows_i, contexts, rows_j = tensor.shape
    rank = pert_factor.shape[1]
    own_j, own_i, slab = rows_j // n_pert, rows_i // n_gene, rank // n_gene
    depth = rows_i * contexts
    width = 256
    f32, bf16 = jnp.float32, jnp.bfloat16
    vmem = pl.BlockSpec(memory_space=pltpu.VMEM)
    return pl.pallas_call(
        functools.partial(sweep, n_pert, n_gene),
        out_shape=(
            jax.ShapeDtypeStruct((rows_j, rank), bf16),
            jax.ShapeDtypeStruct((rows_i, rank), bf16),
        ),
        in_specs=[pl.BlockSpec(memory_space=pl.ANY)] * 3,
        out_specs=(vmem, vmem),
        scratch_shapes=[
            pltpu.VMEM((rows_i, rank), bf16),
            pltpu.VMEM((contexts, rank), bf16),
            pltpu.VMEM((depth, rows_j), bf16),
            pltpu.VMEM((2 * rank, depth), bf16),
            pltpu.VMEM((2 * rank, width), f32),
            pltpu.VMEM((n_gene, slab, rank), f32),
            pltpu.VMEM((2 * n_pert, slab, rank), f32),
            pltpu.VMEM((3 * n_gene, slab, rank), f32),
            pltpu.VMEM((rank, rank), f32),
            pltpu.VMEM((n_pert, own_j, rank), f32),
            pltpu.VMEM((n_pert, own_j, rank), f32),
            pltpu.VMEM((n_pert, own_j, rank), bf16),
            pltpu.VMEM((n_gene, own_i, rank), f32),
            pltpu.VMEM((n_gene, own_i, rank), f32),
            pltpu.VMEM((n_gene, 8, rank), f32),
            pltpu.VMEM((n_pert, 8, rank), f32),
            pltpu.VMEM((n_gene, own_i, rank), bf16),
            pltpu.SemaphoreType.DMA((rows_j // width,)),
            pltpu.SemaphoreType.DMA((2,)),
            pltpu.SemaphoreType.DMA((5, n_pert)),
            pltpu.SemaphoreType.DMA((5, n_pert)),
            pltpu.SemaphoreType.DMA((6, n_gene)),
            pltpu.SemaphoreType.DMA((6, n_gene)),
        ],
        compiler_params=pltpu.CompilerParams(
            collective_id=0, has_side_effects=True, vmem_limit_bytes=64 * 1024 * 1024 - 65536
        ),
        name="sweep",
    )(tensor.reshape(depth, rows_j), pert_factor, context_factor)


def solution(mesh):
    return jax.shard_map(
        functools.partial(shards, mesh.shape["pert"], mesh.shape["gene"]),
        mesh=mesh,
        in_specs=(P("pert", None, "gene"), P("pert", None), P()),
        out_specs=(P("gene", None), P("pert", None)),
        check_vma=False,
    )
```

```python
import functools

import jax
import jax.numpy as jnp
from jax import lax
from jax.experimental import pallas as pl
from jax.experimental.pallas import tpu as pltpu
from jax.sharding import PartitionSpec as P

epsilon = 1e-06
MESH = pl.DeviceIdType.MESH
HIGHEST = lax.Precision.HIGHEST
PANEL = 8


def dot32(a, b, dims):
    return lax.dot_general(
        a, b, (dims, ((), ())), precision=HIGHEST, preferred_element_type=jnp.float32
    )


def reciprocal(x):
    r = pl.reciprocal(x, approx=True)
    r = r * (2.0 - x * r)
    return r * (2.0 - x * r)


def invert_step(a):
    size = a.shape[0]
    lane = lax.broadcasted_iota(jnp.int32, (PANEL, size), 1)
    row = lax.broadcasted_iota(jnp.int32, (PANEL, size), 0)
    rest_lane = lax.broadcasted_iota(jnp.int32, (size - PANEL, size), 1)
    panel = a[:PANEL]
    columns = [jnp.broadcast_to(panel[:, j : j + 1], (PANEL, size)) for j in range(PANEL)]
    for k in range(PANEL):
        inverse = reciprocal(columns[k][k : k + 1])
        pivot = jnp.where(lane[k : k + 1] == k, inverse, panel[k : k + 1] * inverse)
        kept = jnp.where(lane == k, 0.0, panel)
        panel = jnp.where(row == k, pivot, kept - columns[k] * pivot)
        for j in range(k + 1, PANEL):
            head = columns[j][k : k + 1] * inverse
            columns[j] = jnp.where(row == k, head, columns[j] - columns[k] * head)
    shift = size - PANEL
    turned = pltpu.roll(panel, shift, 1)
    rest = a[PANEL:]
    out = pltpu.roll(jnp.where(rest_lane < PANEL, 0.0, rest), shift, 1)
    for j in range(PANEL):
        out = out - rest[:, j : j + 1] * turned[j : j + 1]
    return jnp.concatenate([out, turned], axis=0)


def invert_steps(a, steps):
    return lax.fori_loop(0, steps, lambda _, a: invert_step(a), a)


def sweep(
    n_pert, n_gene, tensor_hbm, factor_ref, context_ref, gene_ref, pert_ref,
    tensor, khatri, product, slab_send, gram_z, gram_g, matrix,
    mttkrp_part, mttkrp_in, mttkrp_all,
    second_part, second_in, squares_g, squares_z, final, load_sem,
    z_send, z_recv, g_send, g_recv,
):
    z = lax.axis_index("pert")
    g = lax.axis_index("gene")
    rows_i, rank = factor_ref.shape
    contexts = context_ref.shape[0]
    depth, rows_j = tensor.shape
    own_j = rows_j // n_pert
    own_i = rows_i // n_gene
    slab = rank // n_gene
    blocks, width = load_sem.shape[0], rows_j // load_sem.shape[0]
    per_block = width // own_j
    gene_count = rows_j * n_gene
    pert_count = rows_i * n_pert

    def z_copy(stage, src, dst, peer):
        return pltpu.make_async_remote_copy(
            src_ref=src, dst_ref=dst.at[z], send_sem=z_send.at[stage, peer],
            recv_sem=z_recv.at[stage, z], device_id=(peer, g), device_id_type=MESH,
        )

    def g_copy(stage, src, dst, peer):
        return pltpu.make_async_remote_copy(
            src_ref=src, dst_ref=dst.at[g], send_sem=g_send.at[stage, peer],
            recv_sem=g_recv.at[stage, g], device_id=(z, peer), device_id_type=MESH,
        )

    def z_wait(stage, dst):
        for d in range(1, n_pert):
            peer = lax.rem(z + d, n_pert)
            pltpu.make_async_remote_copy(
                src_ref=dst.at[peer], dst_ref=dst.at[peer], send_sem=z_send.at[stage, peer],
                recv_sem=z_recv.at[stage, peer], device_id=(peer, g), device_id_type=MESH,
            ).wait_recv()

    def g_wait(stage, dst):
        for d in range(1, n_gene):
            peer = lax.rem(g + d, n_gene)
            pltpu.make_async_remote_copy(
                src_ref=dst.at[peer], dst_ref=dst.at[peer], send_sem=g_send.at[stage, peer],
                recv_sem=g_recv.at[stage, peer], device_id=(z, peer), device_id_type=MESH,
            ).wait_recv()

    z_peers = [lax.rem(z + d, n_pert) for d in range(1, n_pert)]
    g_peers = [lax.rem(g + d, n_gene) for d in range(1, n_gene)]
    sent = []

    def send(copy):
        copy.start()
        sent.append(copy)

    barrier = pltpu.get_barrier_semaphore()
    for peer in z_peers:
        pl.semaphore_signal(barrier, inc=1, device_id=(peer, g), device_id_type=MESH)
    for peer in g_peers:
        pl.semaphore_signal(barrier, inc=1, device_id=(z, peer), device_id_type=MESH)

    def load(block):
        columns = pl.ds(pl.multiple_of(block * width, width), width)
        return pltpu.make_async_copy(
            tensor_hbm.at[:, columns], tensor.at[:, columns], load_sem.at[block]
        )

    order = [lax.rem(z // per_block + 1 + t, blocks) for t in range(blocks)]
    for block in order:
        load(block).start()

    factor = factor_ref[...]
    context = context_ref[...]
    context32 = context.astype(jnp.float32)
    gram_b = lax.dot_general(
        context, context, (((0,), (0,)), ((), ())), preferred_element_type=jnp.float32
    )
    gram = lax.dot_general(
        factor, factor, (((0,), (0,)), ((), ())), preferred_element_type=jnp.float32
    )
    for s in range(n_gene):
        slab_send[s] = gram[s * slab : (s + 1) * slab]
    pl.semaphore_wait(barrier, n_pert + n_gene - 2)

    gram_z[z] = slab_send[g]
    for peer in z_peers:
        send(z_copy(0, gram_z.at[z], gram_z, peer))

    step_i = 128
    step_p = step_i * contexts
    repeat = (
        lax.broadcasted_iota(jnp.int32, (step_i, step_p), 1) // contexts
        == lax.broadcasted_iota(jnp.int32, (step_i, step_p), 0)
    ).astype(jnp.bfloat16)
    cycle = (
        lax.rem(lax.broadcasted_iota(jnp.int32, (contexts, step_p), 1), contexts)
        == lax.broadcasted_iota(jnp.int32, (contexts, step_p), 0)
    ).astype(jnp.bfloat16)
    context_rows = lax.dot_general(
        context, cycle, (((0,), (0,)), ((), ())), preferred_element_type=jnp.float32
    )

    for t in range(rows_i // step_i):
        both = context_rows * lax.dot_general(
            factor_ref[t * step_i : (t + 1) * step_i, :], repeat, (((0,), (0,)), ((), ())),
            preferred_element_type=jnp.float32,
        )
        high = both.astype(jnp.bfloat16)
        khatri[:rank, t * step_p : (t + 1) * step_p] = high
        khatri[rank:, t * step_p : (t + 1) * step_p] = (
            both - high.astype(jnp.float32)
        ).astype(jnp.bfloat16)

    z_wait(0, gram_z)
    total = gram_z[0]
    for s in range(1, n_pert):
        total = total + gram_z[s]
    gram_g[g] = total
    for peer in g_peers:
        send(g_copy(0, gram_g.at[g], gram_g, peer))

    step_d = 2048
    chunks = depth // step_d
    steps = rank // PANEL
    early = min(2, steps // chunks)

    def multiply(c, columns):
        here = pl.ds(pl.multiple_of(c * step_d, step_d), step_d)
        product[...] += jnp.dot(
            khatri[:, here], tensor[here, columns], preferred_element_type=jnp.float32
        )

    for t, block in enumerate(order):
        load(block).wait()
        columns = pl.ds(pl.multiple_of(block * width, width), width)
        product[...] = jnp.zeros_like(product)
        if t < blocks - 1:
            lax.fori_loop(0, chunks, lambda c, carry: (multiply(c, columns), carry)[1], 0)
        else:
            g_wait(0, gram_g)
            for s in range(n_gene):
                matrix[s * slab : (s + 1) * slab, :] = gram_g[s]

            def both_steps(c, inverse):
                multiply(c, columns)
                for _ in range(early):
                    inverse = invert_step(inverse)
                return inverse

            inverse = lax.fori_loop(0, chunks, both_steps, matrix[...] * gram_b)
        turned = (product[:rank] + product[rank:]).T
        for q in range(per_block):
            owner = block * per_block + q
            mttkrp_part[owner] = turned[q * own_j : (q + 1) * own_j]

            @pl.when(owner != z)
            def _():
                z_copy(1, mttkrp_part.at[owner], mttkrp_in, owner).start()

    mttkrp_in[z] = mttkrp_part[z]
    for peer in z_peers:
        sent.append(z_copy(1, mttkrp_part.at[peer], mttkrp_in, peer))

    left = steps - early * chunks
    tail = left // 4
    inverse = invert_steps(inverse, left - 2 * tail)
    z_wait(1, mttkrp_in)
    total = mttkrp_in[0]
    for s in range(1, n_pert):
        total = total + mttkrp_in[s]
    mttkrp_all[z] = total
    gram = dot32(total, total, ((0,), (0,)))
    for s in range(n_gene):
        slab_send[s] = gram[s * slab : (s + 1) * slab]
    gram_in, gram_out = gram_g.at[n_gene : 2 * n_gene], gram_g.at[2 * n_gene : 3 * n_gene]
    slab_z = gram_z.at[n_pert : 2 * n_pert]
    gram_in[g] = slab_send[g]
    for peer in g_peers:
        send(g_copy(1, slab_send.at[peer], gram_in, peer))
    for peer in z_peers:
        send(z_copy(4, mttkrp_all.at[z], mttkrp_all, peer))
    inverse = invert_steps(inverse, tail)
    g_wait(1, gram_in)
    total = gram_in[0]
    for s in range(1, n_gene):
        total = total + gram_in[s]
    slab_z[z] = total
    for peer in z_peers:
        send(z_copy(2, slab_z.at[z], slab_z, peer))
    inverse = invert_steps(inverse, tail)
    z_wait(2, slab_z)
    total = slab_z[0]
    for s in range(1, n_pert):
        total = total + slab_z[s]
    gram_out[g] = total
    for peer in g_peers:
        send(g_copy(2, gram_out.at[g], gram_out, peer))
    z_wait(4, mttkrp_all)
    solved = dot32(mttkrp_all[...].reshape(rows_j, rank), inverse, ((1,), (0,)))
    g_wait(2, gram_out)
    for s in range(n_gene):
        matrix[s * slab : (s + 1) * slab, :] = gram_out[s]
    gram_s = dot32(dot32(inverse, matrix[...], ((0,), (0,))), inverse, ((1,), (0,)))

    diagonal = lax.broadcasted_iota(jnp.int32, (rank, rank), 0) == lax.broadcasted_iota(
        jnp.int32, (rank, rank), 1
    )
    on_diagonal = jnp.where(diagonal, gram_s, 0.0)
    scale_row = jnp.sqrt(jnp.sum(on_diagonal, axis=0, keepdims=True) / gene_count + epsilon)
    scale_column = jnp.sqrt(jnp.sum(on_diagonal, axis=1, keepdims=True) / gene_count + epsilon)
    gene_ref[...] = (solved / scale_row).astype(jnp.bfloat16)
    gram_pert_mode = gram_s / (scale_column * scale_row) * gram_b

    def second(peer):
        here = pl.ds(pl.multiple_of(peer * own_i * contexts, own_i * contexts), own_i * contexts)
        partial = jnp.dot(tensor[here, :], gene_ref[...], preferred_element_type=jnp.float32)
        return jnp.sum(partial.reshape(own_i, contexts, rank) * context32[None], axis=1)

    beside = steps // n_gene

    def second_step(t, inverse):
        peer = lax.rem(g + 1 + t, n_gene)
        second_part[peer] = second(peer)
        g_copy(3, second_part.at[peer], second_in, peer).start()
        for _ in range(beside):
            inverse = invert_step(inverse)
        return inverse

    inverse = lax.fori_loop(0, n_gene - 1, second_step, gram_pert_mode)
    second_in[g] = second(g)
    for peer in g_peers:
        sent.append(g_copy(3, second_part.at[peer], second_in, peer))
    inverse = invert_steps(inverse, steps - beside * (n_gene - 1))
    g_wait(3, second_in)
    total = second_in[0]
    for s in range(1, n_gene):
        total = total + second_in[s]
    solved = dot32(total, inverse, ((1,), (0,)))

    squares_g[g] = jnp.sum((solved * solved).reshape(own_i // 8, 8, rank), axis=0)
    for peer in g_peers:
        send(g_copy(4, squares_g.at[g], squares_g, peer))
    final[g] = solved
    for peer in g_peers:
        send(g_copy(5, final.at[g], final, peer))
    g_wait(4, squares_g)
    total = squares_g[0]
    for s in range(1, n_gene):
        total = total + squares_g[s]
    squares_z[z] = total
    for peer in z_peers:
        send(z_copy(3, squares_z.at[z], squares_z, peer))
    z_wait(3, squares_z)
    total = squares_z[0]
    for s in range(1, n_pert):
        total = total + squares_z[s]
    scale = jnp.sqrt(jnp.sum(total, axis=0, keepdims=True) / pert_count + epsilon)
    g_wait(5, final)
    for s in range(n_gene):
        pert_ref[s * own_i : (s + 1) * own_i, :] = (final[s] / scale).astype(jnp.bfloat16)
    for copy in sent:
        copy.wait_send()


def shards(n_pert, n_gene, tensor, pert_factor, context_factor):
    rows_i, contexts, rows_j = tensor.shape
    rank = pert_factor.shape[1]
    own_j, own_i, slab = rows_j // n_pert, rows_i // n_gene, rank // n_gene
    depth = rows_i * contexts
    width = 256
    f32, bf16 = jnp.float32, jnp.bfloat16
    vmem = pl.BlockSpec(memory_space=pltpu.VMEM)
    return pl.pallas_call(
        functools.partial(sweep, n_pert, n_gene),
        out_shape=(
            jax.ShapeDtypeStruct((rows_j, rank), bf16),
            jax.ShapeDtypeStruct((rows_i, rank), bf16),
        ),
        in_specs=[pl.BlockSpec(memory_space=pl.ANY), vmem, vmem],
        out_specs=(vmem, vmem),
        scratch_shapes=[
            pltpu.VMEM((depth, rows_j), bf16),
            pltpu.VMEM((2 * rank, depth), bf16),
            pltpu.VMEM((2 * rank, width), f32),
            pltpu.VMEM((n_gene, slab, rank), f32),
            pltpu.VMEM((2 * n_pert, slab, rank), f32),
            pltpu.VMEM((3 * n_gene, slab, rank), f32),
            pltpu.VMEM((rank, rank), f32),
            pltpu.VMEM((n_pert, own_j, rank), f32),
            pltpu.VMEM((n_pert, own_j, rank), f32),
            pltpu.VMEM((n_pert, own_j, rank), f32),
            pltpu.VMEM((n_gene, own_i, rank), f32),
            pltpu.VMEM((n_gene, own_i, rank), f32),
            pltpu.VMEM((n_gene, 8, rank), f32),
            pltpu.VMEM((n_pert, 8, rank), f32),
            pltpu.VMEM((n_gene, own_i, rank), f32),
            pltpu.SemaphoreType.DMA((rows_j // width,)),
            pltpu.SemaphoreType.DMA((5, n_pert)),
            pltpu.SemaphoreType.DMA((5, n_pert)),
            pltpu.SemaphoreType.DMA((6, n_gene)),
            pltpu.SemaphoreType.DMA((6, n_gene)),
        ],
        compiler_params=pltpu.CompilerParams(
            collective_id=0, has_side_effects=True, vmem_limit_bytes=48 * 1024 * 1024
        ),
        name="sweep",
    )(tensor.reshape(depth, rows_j), pert_factor, context_factor)


def solution(mesh):
    return jax.shard_map(
        functools.partial(shards, mesh.shape["pert"], mesh.shape["gene"]),
        mesh=mesh,
        in_specs=(P("pert", None, "gene"), P("pert", None), P()),
        out_specs=(P("gene", None), P("pert", None)),
        check_vma=False,
    )
```

```python
import functools

import jax
import jax.numpy as jnp
from jax import lax
from jax.experimental import pallas as pl
from jax.experimental.pallas import tpu as pltpu
from jax.sharding import PartitionSpec as P

epsilon = 1e-06
MESH = pl.DeviceIdType.MESH
HIGHEST = lax.Precision.HIGHEST
PANEL = 8


def dot32(a, b, dims):
    return lax.dot_general(
        a, b, (dims, ((), ())), precision=HIGHEST, preferred_element_type=jnp.float32
    )


def reciprocal(x):
    r = pl.reciprocal(x, approx=True)
    r = r * (2.0 - x * r)
    return r * (2.0 - x * r)


def invert_step(a):
    size = a.shape[0]
    lane = lax.broadcasted_iota(jnp.int32, (PANEL, size), 1)
    row = lax.broadcasted_iota(jnp.int32, (PANEL, size), 0)
    rest_lane = lax.broadcasted_iota(jnp.int32, (size - PANEL, size), 1)
    panel = a[:PANEL]
    columns = [jnp.broadcast_to(panel[:, j : j + 1], (PANEL, size)) for j in range(PANEL)]
    for k in range(PANEL):
        inverse = reciprocal(columns[k][k : k + 1])
        pivot = jnp.where(lane[k : k + 1] == k, inverse, panel[k : k + 1] * inverse)
        kept = jnp.where(lane == k, 0.0, panel)
        panel = jnp.where(row == k, pivot, kept - columns[k] * pivot)
        for j in range(k + 1, PANEL):
            head = columns[j][k : k + 1] * inverse
            columns[j] = jnp.where(row == k, head, columns[j] - columns[k] * head)
    shift = size - PANEL
    turned = pltpu.roll(panel, shift, 1)
    rest = a[PANEL:]
    out = pltpu.roll(jnp.where(rest_lane < PANEL, 0.0, rest), shift, 1)
    for j in range(PANEL):
        out = out - rest[:, j : j + 1] * turned[j : j + 1]
    return jnp.concatenate([out, turned], axis=0)


def invert_steps(a, steps):
    return lax.fori_loop(0, steps, lambda _, a: invert_step(a), a)


def sweep(
    n_pert, n_gene, tensor_hbm, factor_ref, context_ref, gene_ref, pert_ref,
    tensor, khatri, product, slab_send, gram_z, gram_g, matrix,
    mttkrp_part, mttkrp_in, mttkrp_all,
    second_part, second_in, squares_g, squares_z, final, load_sem,
    z_send, z_recv, g_send, g_recv,
):
    z = lax.axis_index("pert")
    g = lax.axis_index("gene")
    rows_i, rank = factor_ref.shape
    contexts = context_ref.shape[0]
    depth, rows_j = tensor.shape
    own_j = rows_j // n_pert
    own_i = rows_i // n_gene
    slab = rank // n_gene
    blocks, width = load_sem.shape[0], rows_j // load_sem.shape[0]
    per_block = width // own_j
    gene_count = rows_j * n_gene
    pert_count = rows_i * n_pert

    def z_copy(stage, src, dst, peer):
        return pltpu.make_async_remote_copy(
            src_ref=src, dst_ref=dst.at[z], send_sem=z_send.at[stage, peer],
            recv_sem=z_recv.at[stage, z], device_id=(peer, g), device_id_type=MESH,
        )

    def g_copy(stage, src, dst, peer):
        return pltpu.make_async_remote_copy(
            src_ref=src, dst_ref=dst.at[g], send_sem=g_send.at[stage, peer],
            recv_sem=g_recv.at[stage, g], device_id=(z, peer), device_id_type=MESH,
        )

    def z_wait(stage, dst):
        for d in range(1, n_pert):
            peer = lax.rem(z + d, n_pert)
            pltpu.make_async_remote_copy(
                src_ref=dst.at[peer], dst_ref=dst.at[peer], send_sem=z_send.at[stage, peer],
                recv_sem=z_recv.at[stage, peer], device_id=(peer, g), device_id_type=MESH,
            ).wait_recv()

    def g_wait(stage, dst):
        for d in range(1, n_gene):
            peer = lax.rem(g + d, n_gene)
            pltpu.make_async_remote_copy(
                src_ref=dst.at[peer], dst_ref=dst.at[peer], send_sem=g_send.at[stage, peer],
                recv_sem=g_recv.at[stage, peer], device_id=(z, peer), device_id_type=MESH,
            ).wait_recv()

    z_peers = [lax.rem(z + d, n_pert) for d in range(1, n_pert)]
    g_peers = [lax.rem(g + d, n_gene) for d in range(1, n_gene)]
    sent = []

    def send(copy):
        copy.start()
        sent.append(copy)

    barrier = pltpu.get_barrier_semaphore()
    for peer in z_peers:
        pl.semaphore_signal(barrier, inc=1, device_id=(peer, g), device_id_type=MESH)
    for peer in g_peers:
        pl.semaphore_signal(barrier, inc=1, device_id=(z, peer), device_id_type=MESH)

    def load(block):
        columns = pl.ds(pl.multiple_of(block * width, width), width)
        return pltpu.make_async_copy(
            tensor_hbm.at[:, columns], tensor.at[:, columns], load_sem.at[block]
        )

    order = [lax.rem(z // per_block + 1 + t, blocks) for t in range(blocks)]
    for block in order:
        load(block).start()

    factor = factor_ref[...]
    context = context_ref[...]
    context32 = context.astype(jnp.float32)
    gram_b = lax.dot_general(
        context, context, (((0,), (0,)), ((), ())), preferred_element_type=jnp.float32
    )
    gram = lax.dot_general(
        factor, factor, (((0,), (0,)), ((), ())), preferred_element_type=jnp.float32
    )
    for s in range(n_gene):
        slab_send[s] = gram[s * slab : (s + 1) * slab]
    pl.semaphore_wait(barrier, n_pert + n_gene - 2)

    gram_z[z] = slab_send[g]
    for peer in z_peers:
        send(z_copy(0, gram_z.at[z], gram_z, peer))

    step_i = 128
    step_p = step_i * contexts
    repeat = (
        lax.broadcasted_iota(jnp.int32, (step_i, step_p), 1) // contexts
        == lax.broadcasted_iota(jnp.int32, (step_i, step_p), 0)
    ).astype(jnp.bfloat16)
    cycle = (
        lax.rem(lax.broadcasted_iota(jnp.int32, (contexts, step_p), 1), contexts)
        == lax.broadcasted_iota(jnp.int32, (contexts, step_p), 0)
    ).astype(jnp.bfloat16)
    context_rows = lax.dot_general(
        context, cycle, (((0,), (0,)), ((), ())), preferred_element_type=jnp.float32
    )

    for t in range(rows_i // step_i):
        both = context_rows * lax.dot_general(
            factor_ref[t * step_i : (t + 1) * step_i, :], repeat, (((0,), (0,)), ((), ())),
            preferred_element_type=jnp.float32,
        )
        high = both.astype(jnp.bfloat16)
        khatri[:rank, t * step_p : (t + 1) * step_p] = high
        khatri[rank:, t * step_p : (t + 1) * step_p] = (
            both - high.astype(jnp.float32)
        ).astype(jnp.bfloat16)

    z_wait(0, gram_z)
    total = gram_z[0]
    for s in range(1, n_pert):
        total = total + gram_z[s]
    gram_g[g] = total
    for peer in g_peers:
        send(g_copy(0, gram_g.at[g], gram_g, peer))

    step_d = 2048
    chunks = depth // step_d
    steps = rank // PANEL
    early = min(2, steps // chunks)

    def multiply(c, columns):
        here = pl.ds(pl.multiple_of(c * step_d, step_d), step_d)
        product[...] += jnp.dot(
            khatri[:, here], tensor[here, columns], preferred_element_type=jnp.float32
        )

    for t, block in enumerate(order):
        load(block).wait()
        columns = pl.ds(pl.multiple_of(block * width, width), width)
        product[...] = jnp.zeros_like(product)
        if t < blocks - 1:
            lax.fori_loop(0, chunks, lambda c, carry: (multiply(c, columns), carry)[1], 0)
        else:
            g_wait(0, gram_g)
            for s in range(n_gene):
                matrix[s * slab : (s + 1) * slab, :] = gram_g[s]

            def both_steps(c, inverse):
                multiply(c, columns)
                for _ in range(early):
                    inverse = invert_step(inverse)
                return inverse

            inverse = lax.fori_loop(0, chunks, both_steps, matrix[...] * gram_b)
        turned = (product[:rank] + product[rank:]).T
        for q in range(per_block):
            owner = block * per_block + q
            mttkrp_part[owner] = turned[q * own_j : (q + 1) * own_j]

            @pl.when(owner != z)
            def _():
                z_copy(1, mttkrp_part.at[owner], mttkrp_in, owner).start()

    mttkrp_in[z] = mttkrp_part[z]
    for peer in z_peers:
        sent.append(z_copy(1, mttkrp_part.at[peer], mttkrp_in, peer))

    left = steps - early * chunks
    tail = left // 4
    inverse = invert_steps(inverse, left - 2 * tail)
    z_wait(1, mttkrp_in)
    total = mttkrp_in[0]
    for s in range(1, n_pert):
        total = total + mttkrp_in[s]
    mttkrp_all[z] = total
    gram = dot32(total, total, ((0,), (0,)))
    for s in range(n_gene):
        slab_send[s] = gram[s * slab : (s + 1) * slab]
    gram_in, gram_out = gram_g.at[n_gene : 2 * n_gene], gram_g.at[2 * n_gene : 3 * n_gene]
    slab_z = gram_z.at[n_pert : 2 * n_pert]
    gram_in[g] = slab_send[g]
    for peer in g_peers:
        send(g_copy(1, slab_send.at[peer], gram_in, peer))
    for peer in z_peers:
        send(z_copy(4, mttkrp_all.at[z], mttkrp_all, peer))
    inverse = invert_steps(inverse, tail)
    g_wait(1, gram_in)
    total = gram_in[0]
    for s in range(1, n_gene):
        total = total + gram_in[s]
    slab_z[z] = total
    for peer in z_peers:
        send(z_copy(2, slab_z.at[z], slab_z, peer))
    inverse = invert_steps(inverse, tail)
    z_wait(2, slab_z)
    total = slab_z[0]
    for s in range(1, n_pert):
        total = total + slab_z[s]
    gram_out[g] = total
    for peer in g_peers:
        send(g_copy(2, gram_out.at[g], gram_out, peer))
    z_wait(4, mttkrp_all)
    solved = dot32(mttkrp_all[...].reshape(rows_j, rank), inverse, ((1,), (0,)))
    g_wait(2, gram_out)
    for s in range(n_gene):
        matrix[s * slab : (s + 1) * slab, :] = gram_out[s]
    gram_s = dot32(dot32(inverse, matrix[...], ((0,), (0,))), inverse, ((1,), (0,)))

    diagonal = lax.broadcasted_iota(jnp.int32, (rank, rank), 0) == lax.broadcasted_iota(
        jnp.int32, (rank, rank), 1
    )
    on_diagonal = jnp.where(diagonal, gram_s, 0.0)
    scale_row = jnp.sqrt(jnp.sum(on_diagonal, axis=0, keepdims=True) / gene_count + epsilon)
    scale_column = jnp.sqrt(jnp.sum(on_diagonal, axis=1, keepdims=True) / gene_count + epsilon)
    gene_ref[...] = (solved / scale_row).astype(jnp.bfloat16)
    gram_pert_mode = gram_s / (scale_column * scale_row) * gram_b

    add_contexts = (
        lax.broadcasted_iota(jnp.int32, (own_i, own_i * contexts), 1) // contexts
        == lax.broadcasted_iota(jnp.int32, (own_i, own_i * contexts), 0)
    ).astype(jnp.bfloat16)

    def second(peer):
        here = pl.ds(pl.multiple_of(peer * own_i * contexts, own_i * contexts), own_i * contexts)
        partial = jnp.dot(tensor[here, :], gene_ref[...], preferred_element_type=jnp.float32)
        terms = partial.reshape(own_i, contexts, rank) * context32[None]
        terms = terms.reshape(own_i * contexts, rank)
        high = terms.astype(jnp.bfloat16)
        low = (terms - high.astype(jnp.float32)).astype(jnp.bfloat16)
        both = jnp.dot(
            add_contexts, jnp.concatenate([high, low], axis=1), preferred_element_type=jnp.float32
        )
        return both[:, :rank] + both[:, rank:]

    beside = steps // n_gene

    def second_step(t, inverse):
        peer = lax.rem(g + 1 + t, n_gene)
        second_part[peer] = second(peer)
        g_copy(3, second_part.at[peer], second_in, peer).start()
        for _ in range(beside):
            inverse = invert_step(inverse)
        return inverse

    inverse = lax.fori_loop(0, n_gene - 1, second_step, gram_pert_mode)
    second_in[g] = second(g)
    for peer in g_peers:
        sent.append(g_copy(3, second_part.at[peer], second_in, peer))
    inverse = invert_steps(inverse, steps - beside * (n_gene - 1))
    g_wait(3, second_in)
    total = second_in[0]
    for s in range(1, n_gene):
        total = total + second_in[s]
    solved = dot32(total, inverse, ((1,), (0,)))

    squares_g[g] = jnp.sum((solved * solved).reshape(own_i // 8, 8, rank), axis=0)
    for peer in g_peers:
        send(g_copy(4, squares_g.at[g], squares_g, peer))
    final[g] = solved
    for peer in g_peers:
        send(g_copy(5, final.at[g], final, peer))
    g_wait(4, squares_g)
    total = squares_g[0]
    for s in range(1, n_gene):
        total = total + squares_g[s]
    squares_z[z] = total
    for peer in z_peers:
        send(z_copy(3, squares_z.at[z], squares_z, peer))
    z_wait(3, squares_z)
    total = squares_z[0]
    for s in range(1, n_pert):
        total = total + squares_z[s]
    scale = jnp.sqrt(jnp.sum(total, axis=0, keepdims=True) / pert_count + epsilon)
    g_wait(5, final)
    for s in range(n_gene):
        pert_ref[s * own_i : (s + 1) * own_i, :] = (final[s] / scale).astype(jnp.bfloat16)
    for copy in sent:
        copy.wait_send()


def shards(n_pert, n_gene, tensor, pert_factor, context_factor):
    rows_i, contexts, rows_j = tensor.shape
    rank = pert_factor.shape[1]
    own_j, own_i, slab = rows_j // n_pert, rows_i // n_gene, rank // n_gene
    depth = rows_i * contexts
    width = 256
    f32, bf16 = jnp.float32, jnp.bfloat16
    vmem = pl.BlockSpec(memory_space=pltpu.VMEM)
    return pl.pallas_call(
        functools.partial(sweep, n_pert, n_gene),
        out_shape=(
            jax.ShapeDtypeStruct((rows_j, rank), bf16),
            jax.ShapeDtypeStruct((rows_i, rank), bf16),
        ),
        in_specs=[pl.BlockSpec(memory_space=pl.ANY), vmem, vmem],
        out_specs=(vmem, vmem),
        scratch_shapes=[
            pltpu.VMEM((depth, rows_j), bf16),
            pltpu.VMEM((2 * rank, depth), bf16),
            pltpu.VMEM((2 * rank, width), f32),
            pltpu.VMEM((n_gene, slab, rank), f32),
            pltpu.VMEM((2 * n_pert, slab, rank), f32),
            pltpu.VMEM((3 * n_gene, slab, rank), f32),
            pltpu.VMEM((rank, rank), f32),
            pltpu.VMEM((n_pert, own_j, rank), f32),
            pltpu.VMEM((n_pert, own_j, rank), f32),
            pltpu.VMEM((n_pert, own_j, rank), f32),
            pltpu.VMEM((n_gene, own_i, rank), f32),
            pltpu.VMEM((n_gene, own_i, rank), f32),
            pltpu.VMEM((n_gene, 8, rank), f32),
            pltpu.VMEM((n_pert, 8, rank), f32),
            pltpu.VMEM((n_gene, own_i, rank), f32),
            pltpu.SemaphoreType.DMA((rows_j // width,)),
            pltpu.SemaphoreType.DMA((5, n_pert)),
            pltpu.SemaphoreType.DMA((5, n_pert)),
            pltpu.SemaphoreType.DMA((6, n_gene)),
            pltpu.SemaphoreType.DMA((6, n_gene)),
        ],
        compiler_params=pltpu.CompilerParams(
            collective_id=0, has_side_effects=True, vmem_limit_bytes=48 * 1024 * 1024
        ),
        name="sweep",
    )(tensor.reshape(depth, rows_j), pert_factor, context_factor)


def solution(mesh):
    return jax.shard_map(
        functools.partial(shards, mesh.shape["pert"], mesh.shape["gene"]),
        mesh=mesh,
        in_specs=(P("pert", None, "gene"), P("pert", None), P()),
        out_specs=(P("gene", None), P("pert", None)),
        check_vma=False,
    )
```

```python
import functools

import jax
import jax.numpy as jnp
from jax import lax
from jax.experimental import pallas as pl
from jax.experimental.pallas import tpu as pltpu
from jax.sharding import PartitionSpec as P

epsilon = 1e-06
MESH = pl.DeviceIdType.MESH
HIGHEST = lax.Precision.HIGHEST
PANEL = 8


def dot32(a, b, dims):
    return lax.dot_general(
        a, b, (dims, ((), ())), precision=HIGHEST, preferred_element_type=jnp.float32
    )


def reciprocal(x):
    r = pl.reciprocal(x, approx=True)
    r = r * (2.0 - x * r)
    return r * (2.0 - x * r)


def invert_step(a):
    size = a.shape[0]
    lane = lax.broadcasted_iota(jnp.int32, (PANEL, size), 1)
    row = lax.broadcasted_iota(jnp.int32, (PANEL, size), 0)
    rest_lane = lax.broadcasted_iota(jnp.int32, (size - PANEL, size), 1)
    panel = a[:PANEL]
    columns = [jnp.broadcast_to(panel[:, j : j + 1], (PANEL, size)) for j in range(PANEL)]
    for k in range(PANEL):
        inverse = reciprocal(columns[k][k : k + 1])
        pivot = jnp.where(lane[k : k + 1] == k, inverse, panel[k : k + 1] * inverse)
        kept = jnp.where(lane == k, 0.0, panel)
        panel = jnp.where(row == k, pivot, kept - columns[k] * pivot)
        for j in range(k + 1, PANEL):
            head = columns[j][k : k + 1] * inverse
            columns[j] = jnp.where(row == k, head, columns[j] - columns[k] * head)
    shift = size - PANEL
    turned = pltpu.roll(panel, shift, 1)
    rest = a[PANEL:]
    out = pltpu.roll(jnp.where(rest_lane < PANEL, 0.0, rest), shift, 1)
    out = out - dot32(rest[:, :PANEL], turned, ((1,), (0,)))
    return jnp.concatenate([out, turned], axis=0)


def invert_steps(a, steps):
    return lax.fori_loop(0, steps, lambda _, a: invert_step(a), a)


def sweep(
    n_pert, n_gene, tensor_hbm, factor_ref, context_ref, gene_ref, pert_ref,
    tensor, khatri, product, slab_send, gram_z, gram_g, matrix,
    mttkrp_part, mttkrp_in, mttkrp_all,
    second_part, second_in, squares_g, squares_z, final, load_sem,
    z_send, z_recv, g_send, g_recv,
):
    z = lax.axis_index("pert")
    g = lax.axis_index("gene")
    rows_i, rank = factor_ref.shape
    contexts = context_ref.shape[0]
    depth, rows_j = tensor.shape
    own_j = rows_j // n_pert
    own_i = rows_i // n_gene
    slab = rank // n_gene
    blocks, width = load_sem.shape[0], rows_j // load_sem.shape[0]
    per_block = width // own_j
    gene_count = rows_j * n_gene
    pert_count = rows_i * n_pert

    def z_copy(stage, src, dst, peer):
        return pltpu.make_async_remote_copy(
            src_ref=src, dst_ref=dst.at[z], send_sem=z_send.at[stage, peer],
            recv_sem=z_recv.at[stage, z], device_id=(peer, g), device_id_type=MESH,
        )

    def g_copy(stage, src, dst, peer):
        return pltpu.make_async_remote_copy(
            src_ref=src, dst_ref=dst.at[g], send_sem=g_send.at[stage, peer],
            recv_sem=g_recv.at[stage, g], device_id=(z, peer), device_id_type=MESH,
        )

    def z_wait(stage, dst):
        for d in range(1, n_pert):
            peer = lax.rem(z + d, n_pert)
            pltpu.make_async_remote_copy(
                src_ref=dst.at[peer], dst_ref=dst.at[peer], send_sem=z_send.at[stage, peer],
                recv_sem=z_recv.at[stage, peer], device_id=(peer, g), device_id_type=MESH,
            ).wait_recv()

    def g_wait(stage, dst):
        for d in range(1, n_gene):
            peer = lax.rem(g + d, n_gene)
            pltpu.make_async_remote_copy(
                src_ref=dst.at[peer], dst_ref=dst.at[peer], send_sem=g_send.at[stage, peer],
                recv_sem=g_recv.at[stage, peer], device_id=(z, peer), device_id_type=MESH,
            ).wait_recv()

    z_peers = [lax.rem(z + d, n_pert) for d in range(1, n_pert)]
    g_peers = [lax.rem(g + d, n_gene) for d in range(1, n_gene)]
    sent = []

    def send(copy):
        copy.start()
        sent.append(copy)

    barrier = pltpu.get_barrier_semaphore()
    for peer in z_peers:
        pl.semaphore_signal(barrier, inc=1, device_id=(peer, g), device_id_type=MESH)
    for peer in g_peers:
        pl.semaphore_signal(barrier, inc=1, device_id=(z, peer), device_id_type=MESH)

    def load(block):
        columns = pl.ds(pl.multiple_of(block * width, width), width)
        return pltpu.make_async_copy(
            tensor_hbm.at[:, columns], tensor.at[:, columns], load_sem.at[block]
        )

    order = [lax.rem(z // per_block + 1 + t, blocks) for t in range(blocks)]
    for block in order:
        load(block).start()

    factor = factor_ref[...]
    context = context_ref[...]
    context32 = context.astype(jnp.float32)
    gram_b = lax.dot_general(
        context, context, (((0,), (0,)), ((), ())), preferred_element_type=jnp.float32
    )
    gram = lax.dot_general(
        factor, factor, (((0,), (0,)), ((), ())), preferred_element_type=jnp.float32
    )
    for s in range(n_gene):
        slab_send[s] = gram[s * slab : (s + 1) * slab]
    pl.semaphore_wait(barrier, n_pert + n_gene - 2)

    gram_z[z] = slab_send[g]
    for peer in z_peers:
        send(z_copy(0, gram_z.at[z], gram_z, peer))

    step_i = 128
    step_p = step_i * contexts
    repeat = (
        lax.broadcasted_iota(jnp.int32, (step_i, step_p), 1) // contexts
        == lax.broadcasted_iota(jnp.int32, (step_i, step_p), 0)
    ).astype(jnp.bfloat16)
    cycle = (
        lax.rem(lax.broadcasted_iota(jnp.int32, (contexts, step_p), 1), contexts)
        == lax.broadcasted_iota(jnp.int32, (contexts, step_p), 0)
    ).astype(jnp.bfloat16)
    context_rows = lax.dot_general(
        context, cycle, (((0,), (0,)), ((), ())), preferred_element_type=jnp.float32
    )

    for t in range(rows_i // step_i):
        both = context_rows * lax.dot_general(
            factor_ref[t * step_i : (t + 1) * step_i, :], repeat, (((0,), (0,)), ((), ())),
            preferred_element_type=jnp.float32,
        )
        high = both.astype(jnp.bfloat16)
        khatri[:rank, t * step_p : (t + 1) * step_p] = high
        khatri[rank:, t * step_p : (t + 1) * step_p] = (
            both - high.astype(jnp.float32)
        ).astype(jnp.bfloat16)

    z_wait(0, gram_z)
    total = gram_z[0]
    for s in range(1, n_pert):
        total = total + gram_z[s]
    gram_g[g] = total
    for peer in g_peers:
        send(g_copy(0, gram_g.at[g], gram_g, peer))

    step_d = 2048
    chunks = depth // step_d
    steps = rank // PANEL
    early = min(2, steps // chunks)

    def multiply(c, columns):
        here = pl.ds(pl.multiple_of(c * step_d, step_d), step_d)
        product[...] += jnp.dot(
            khatri[:, here], tensor[here, columns], preferred_element_type=jnp.float32
        )

    for t, block in enumerate(order):
        load(block).wait()
        columns = pl.ds(pl.multiple_of(block * width, width), width)
        product[...] = jnp.zeros_like(product)
        if t < blocks - 1:
            lax.fori_loop(0, chunks, lambda c, carry: (multiply(c, columns), carry)[1], 0)
        else:
            g_wait(0, gram_g)
            for s in range(n_gene):
                matrix[s * slab : (s + 1) * slab, :] = gram_g[s]

            def both_steps(c, inverse):
                multiply(c, columns)
                for _ in range(early):
                    inverse = invert_step(inverse)
                return inverse

            inverse = lax.fori_loop(0, chunks, both_steps, matrix[...] * gram_b)
        turned = (product[:rank] + product[rank:]).T
        for q in range(per_block):
            owner = block * per_block + q
            mttkrp_part[owner] = turned[q * own_j : (q + 1) * own_j]

            @pl.when(owner != z)
            def _():
                z_copy(1, mttkrp_part.at[owner], mttkrp_in, owner).start()

    mttkrp_in[z] = mttkrp_part[z]
    for peer in z_peers:
        sent.append(z_copy(1, mttkrp_part.at[peer], mttkrp_in, peer))

    left = steps - early * chunks
    tail = left // 4
    inverse = invert_steps(inverse, left - 2 * tail)
    z_wait(1, mttkrp_in)
    total = mttkrp_in[0]
    for s in range(1, n_pert):
        total = total + mttkrp_in[s]
    mttkrp_all[z] = total
    gram = dot32(total, total, ((0,), (0,)))
    for s in range(n_gene):
        slab_send[s] = gram[s * slab : (s + 1) * slab]
    gram_in, gram_out = gram_g.at[n_gene : 2 * n_gene], gram_g.at[2 * n_gene : 3 * n_gene]
    slab_z = gram_z.at[n_pert : 2 * n_pert]
    gram_in[g] = slab_send[g]
    for peer in g_peers:
        send(g_copy(1, slab_send.at[peer], gram_in, peer))
    for peer in z_peers:
        send(z_copy(4, mttkrp_all.at[z], mttkrp_all, peer))
    inverse = invert_steps(inverse, tail)
    g_wait(1, gram_in)
    total = gram_in[0]
    for s in range(1, n_gene):
        total = total + gram_in[s]
    slab_z[z] = total
    for peer in z_peers:
        send(z_copy(2, slab_z.at[z], slab_z, peer))
    inverse = invert_steps(inverse, tail)
    z_wait(2, slab_z)
    total = slab_z[0]
    for s in range(1, n_pert):
        total = total + slab_z[s]
    gram_out[g] = total
    for peer in g_peers:
        send(g_copy(2, gram_out.at[g], gram_out, peer))
    z_wait(4, mttkrp_all)
    solved = dot32(mttkrp_all[...].reshape(rows_j, rank), inverse, ((1,), (0,)))
    g_wait(2, gram_out)
    for s in range(n_gene):
        matrix[s * slab : (s + 1) * slab, :] = gram_out[s]
    gram_s = dot32(dot32(inverse, matrix[...], ((0,), (0,))), inverse, ((1,), (0,)))

    diagonal = lax.broadcasted_iota(jnp.int32, (rank, rank), 0) == lax.broadcasted_iota(
        jnp.int32, (rank, rank), 1
    )
    on_diagonal = jnp.where(diagonal, gram_s, 0.0)
    scale_row = jnp.sqrt(jnp.sum(on_diagonal, axis=0, keepdims=True) / gene_count + epsilon)
    scale_column = jnp.sqrt(jnp.sum(on_diagonal, axis=1, keepdims=True) / gene_count + epsilon)
    gene_ref[...] = (solved / scale_row).astype(jnp.bfloat16)
    gram_pert_mode = gram_s / (scale_column * scale_row) * gram_b

    add_contexts = (
        lax.broadcasted_iota(jnp.int32, (own_i, own_i * contexts), 1) // contexts
        == lax.broadcasted_iota(jnp.int32, (own_i, own_i * contexts), 0)
    ).astype(jnp.bfloat16)

    def second(peer):
        here = pl.ds(pl.multiple_of(peer * own_i * contexts, own_i * contexts), own_i * contexts)
        partial = jnp.dot(tensor[here, :], gene_ref[...], preferred_element_type=jnp.float32)
        terms = partial.reshape(own_i, contexts, rank) * context32[None]
        terms = terms.reshape(own_i * contexts, rank)
        high = terms.astype(jnp.bfloat16)
        low = (terms - high.astype(jnp.float32)).astype(jnp.bfloat16)
        both = jnp.dot(
            add_contexts, jnp.concatenate([high, low], axis=1), preferred_element_type=jnp.float32
        )
        return both[:, :rank] + both[:, rank:]

    beside = steps // n_gene

    def second_step(t, inverse):
        peer = lax.rem(g + 1 + t, n_gene)
        second_part[peer] = second(peer)
        g_copy(3, second_part.at[peer], second_in, peer).start()
        for _ in range(beside):
            inverse = invert_step(inverse)
        return inverse

    inverse = lax.fori_loop(0, n_gene - 1, second_step, gram_pert_mode)
    second_in[g] = second(g)
    for peer in g_peers:
        sent.append(g_copy(3, second_part.at[peer], second_in, peer))
    inverse = invert_steps(inverse, steps - beside * (n_gene - 1))
    g_wait(3, second_in)
    total = second_in[0]
    for s in range(1, n_gene):
        total = total + second_in[s]
    solved = dot32(total, inverse, ((1,), (0,)))

    squares_g[g] = jnp.sum((solved * solved).reshape(own_i // 8, 8, rank), axis=0)
    for peer in g_peers:
        send(g_copy(4, squares_g.at[g], squares_g, peer))
    final[g] = solved
    for peer in g_peers:
        send(g_copy(5, final.at[g], final, peer))
    g_wait(4, squares_g)
    total = squares_g[0]
    for s in range(1, n_gene):
        total = total + squares_g[s]
    squares_z[z] = total
    for peer in z_peers:
        send(z_copy(3, squares_z.at[z], squares_z, peer))
    z_wait(3, squares_z)
    total = squares_z[0]
    for s in range(1, n_pert):
        total = total + squares_z[s]
    scale = jnp.sqrt(jnp.sum(total, axis=0, keepdims=True) / pert_count + epsilon)
    g_wait(5, final)
    for s in range(n_gene):
        pert_ref[s * own_i : (s + 1) * own_i, :] = (final[s] / scale).astype(jnp.bfloat16)
    for copy in sent:
        copy.wait_send()


def shards(n_pert, n_gene, tensor, pert_factor, context_factor):
    rows_i, contexts, rows_j = tensor.shape
    rank = pert_factor.shape[1]
    own_j, own_i, slab = rows_j // n_pert, rows_i // n_gene, rank // n_gene
    depth = rows_i * contexts
    width = 256
    f32, bf16 = jnp.float32, jnp.bfloat16
    vmem = pl.BlockSpec(memory_space=pltpu.VMEM)
    return pl.pallas_call(
        functools.partial(sweep, n_pert, n_gene),
        out_shape=(
            jax.ShapeDtypeStruct((rows_j, rank), bf16),
            jax.ShapeDtypeStruct((rows_i, rank), bf16),
        ),
        in_specs=[pl.BlockSpec(memory_space=pl.ANY), vmem, vmem],
        out_specs=(vmem, vmem),
        scratch_shapes=[
            pltpu.VMEM((depth, rows_j), bf16),
            pltpu.VMEM((2 * rank, depth), bf16),
            pltpu.VMEM((2 * rank, width), f32),
            pltpu.VMEM((n_gene, slab, rank), f32),
            pltpu.VMEM((2 * n_pert, slab, rank), f32),
            pltpu.VMEM((3 * n_gene, slab, rank), f32),
            pltpu.VMEM((rank, rank), f32),
            pltpu.VMEM((n_pert, own_j, rank), f32),
            pltpu.VMEM((n_pert, own_j, rank), f32),
            pltpu.VMEM((n_pert, own_j, rank), f32),
            pltpu.VMEM((n_gene, own_i, rank), f32),
            pltpu.VMEM((n_gene, own_i, rank), f32),
            pltpu.VMEM((n_gene, 8, rank), f32),
            pltpu.VMEM((n_pert, 8, rank), f32),
            pltpu.VMEM((n_gene, own_i, rank), f32),
            pltpu.SemaphoreType.DMA((rows_j // width,)),
            pltpu.SemaphoreType.DMA((5, n_pert)),
            pltpu.SemaphoreType.DMA((5, n_pert)),
            pltpu.SemaphoreType.DMA((6, n_gene)),
            pltpu.SemaphoreType.DMA((6, n_gene)),
        ],
        compiler_params=pltpu.CompilerParams(
            collective_id=0, has_side_effects=True, vmem_limit_bytes=48 * 1024 * 1024
        ),
        name="sweep",
    )(tensor.reshape(depth, rows_j), pert_factor, context_factor)


def solution(mesh):
    return jax.shard_map(
        functools.partial(shards, mesh.shape["pert"], mesh.shape["gene"]),
        mesh=mesh,
        in_specs=(P("pert", None, "gene"), P("pert", None), P()),
        out_specs=(P("gene", None), P("pert", None)),
        check_vma=False,
    )
```
